256 devices in a mesh: var: 8 (over y_hi, x), lat: 16 (over z, y_lo), dp: 2 (over core).
Axes of the slice: x: 4, y: 4 (y_hi: 2, y_lo: 2; y = y_hi * 2 + y_lo), z: 8, core: 2. Of those that a mesh axis runs over, the one named last changes fastest.
Arguments:
- patches: bfloat16 [16, 96, 7680], P(('dp', 'var'), 'lat'), parts along dimension 0, may hold values from -6 to 6
- level_bias: bfloat16 [8, 512], replicated, may hold values from -6 to 6
- embed_weight: bfloat16 [80, 512], replicated, may hold values from -0.625 to 0.625
- latent_query: bfloat16 [3, 512], replicated, may hold values from -60 to 60
- cross_key: bfloat16 [512, 512], replicated, may hold values from -0.25 to 0.25
- cross_value: bfloat16 [512, 512], replicated, may hold values from -0.25 to 0.25
- cross_output: bfloat16 [512, 512], replicated, may hold values from -0.25 to 0.25
- first_gain: float32 [512], replicated, may hold values from 0.1 to 1.9
- window_query: bfloat16 [512, 512], replicated, may hold values from -2 to 2
- window_context: bfloat16 [512, 1024], replicated, may hold values from -0.25 to 0.25
- window_output: bfloat16 [512, 512], replicated, may hold values from -0.25 to 0.25
- second_gain: float32 [512], replicated, may hold values from 0.1 to 1.9
- up_weight: bfloat16 [512, 2048], replicated, may hold values from -0.25 to 0.25
- down_weight: bfloat16 [2048, 512], replicated, may hold values from -0.125 to 0.125
Outputs:
- encoded: bfloat16 [6, 96, 96, 512], P('dp', 'lat', 'var'), parts along dimension 0
The draws below stay inside these ranges and needn't reach their ends.
There are 2 independent parts, one for each index of `dp`. The reference program is written for one: setup_inputs(seed, part) draws one part's arguments, and reference() takes and returns one part's arrays. A program takes and returns all parts, laid end to end along the dimension named above; an argument that names none is the same for every part. Nothing has to cross between parts.
All inputs are finite; a program needn't handle non-finite values.
Results may differ from the reference program's by a relative error of at most 0.013.
Values may be sent and summed in bfloat16 or wider, within the bound.
No kernel may reach another device: no remote copies, remote signals or barrier semaphores. Data moves between devices by JAX's collectives and lax.ppermute only.
A program may use at most 64 MiB of HBM per device.

```python
import jax
import jax.numpy as jnp
from jax import lax

D = 512
HEADS = 16
MLP_UNITS = 2048
PATCH_IN = 80
LATENT = 3
WLAT = 6
WLON = 12
LEVELS = 8
NLAT = 96
NLON = 96
SHIFT = 3


def draw_latent_query(key, part):
    first_key = jax.random.fold_in(jax.random.fold_in(key, 11), 0)
    entries = jnp.clip(jax.random.normal(first_key, (LATENT, D), jnp.float32), -4.0, 4.0)
    return entries.astype(jnp.bfloat16)


def draw_window_query(key, part):
    first_key = jax.random.fold_in(jax.random.fold_in(key, 23), 0)
    entries = jnp.clip(jax.random.normal(first_key, (D, D), jnp.float32), -4.0, 4.0) * D ** (-0.5)
    return entries.astype(jnp.bfloat16)


def steps_of(key, dims, cuts, low, high):
    gain = 1.0
    for dim, shards_of in cuts:
        steps = jax.random.uniform(jax.random.fold_in(jax.random.fold_in(key, 6), dim), (shards_of,), jnp.float32, low / len(cuts), high / len(cuts))
        gain = gain * jnp.repeat(jnp.exp(steps), dims[dim] // shards_of).reshape((-1,) + (1,) * (len(dims) - 1 - dim))
    return gain


def scatter_about(own_key, extent, scale, reach, shards=(), held_as=jnp.bfloat16):
    values = scale * jax.random.normal(own_key, extent, jnp.float32)
    if shards:
        values = values * steps_of(own_key, extent, shards, -0.22, 0.18)
    return jnp.clip(values, -reach, reach).astype(held_as)


def setup_inputs(seed: int = 0, part: int = 0) -> dict:
    splits = jax.random.split(jax.random.key(seed), 15)
    part_keys = jax.random.split(jax.random.fold_in(splits[14], part), 15)
    return {
        "patches": scatter_about(part_keys[0], (LEVELS, NLAT, NLON * PATCH_IN), 1.0, 6.0, ((0, 8), (1, 16))),
        "level_bias": scatter_about(splits[1], (LEVELS, D), 1.0, 6.0),
        "embed_weight": scatter_about(splits[2], (PATCH_IN, D), PATCH_IN ** -0.5, 0.625),
        "latent_query": draw_latent_query(jax.random.fold_in(splits[14], 71), part),
        "cross_key": scatter_about(splits[4], (D, D), D ** -0.5, 0.25),
        "cross_value": scatter_about(splits[5], (D, D), D ** -0.5, 0.25),
        "cross_output": scatter_about(splits[6], (D, D), D ** -0.5, 0.25),
        "first_gain": jnp.clip(1.0 + 0.18 * jax.random.normal(splits[7], (D,), jnp.float32), 0.1, 1.9),
        "window_query": draw_window_query(jax.random.fold_in(splits[14], 71), part),
        "window_context": scatter_about(splits[9], (D, 2 * D), D ** -0.5, 0.25),
        "window_output": scatter_about(splits[10], (D, D), D ** -0.5, 0.25),
        "second_gain": jnp.clip(1.0 + 0.18 * jax.random.normal(splits[11], (D,), jnp.float32), 0.1, 1.9),
        "up_weight": scatter_about(splits[12], (D, MLP_UNITS), D ** -0.5, 0.25),
        "down_weight": scatter_about(splits[13], (MLP_UNITS, D), MLP_UNITS ** -0.5, 0.125),
    }


epsilon = 1e-05
masked_score = -1e+30

def layer_norm(tensor, scales):
    center = lax.optimization_barrier(jnp.mean(tensor, axis=-1, keepdims=True))
    offset = tensor - center
    spread = lax.optimization_barrier(jnp.mean(offset * offset, axis=-1, keepdims=True))
    return offset * lax.rsqrt(spread + epsilon) * scales.astype(jnp.float32)

def level_partials(pixels, biases, embed_weight, latent_query, cross_key, cross_value):
    level_count, row_count, flat_cols = pixels.shape
    pixel_count, channels = embed_weight.shape
    col_count = flat_cols // pixel_count
    head_size = channels // HEADS
    latent_count = latent_query.shape[0]
    embedded = jnp.dot(pixels.reshape(-1, pixel_count), embed_weight, preferred_element_type=jnp.float32)
    embedded = embedded.reshape(level_count, -1, channels) + biases.astype(jnp.float32)[:, None, :]
    embedded = embedded.astype(jnp.bfloat16).reshape(-1, channels)
    head_shape = (level_count, row_count, col_count, HEADS, head_size)
    key_rows = jnp.dot(embedded, cross_key, preferred_element_type=jnp.float32).astype(jnp.bfloat16).reshape(head_shape)
    value_rows = jnp.dot(embedded, cross_value, preferred_element_type=jnp.float32).astype(jnp.bfloat16).reshape(head_shape)
    queries = latent_query.astype(jnp.float32).reshape(latent_count, HEADS, head_size)
    scores = jnp.einsum('lrwhc,qhc->qrwhl', key_rows.astype(jnp.float32), queries) * head_size ** (-0.5)
    maxima = lax.optimization_barrier(jnp.max(scores, axis=-1))
    weights = jnp.exp(scores - maxima[..., None])
    totals = lax.optimization_barrier(jnp.sum(weights, axis=-1))
    weighted = jnp.einsum('qrwhl,lrwhc->qrwhc', weights, value_rows.astype(jnp.float32), precision=lax.Precision.HIGHEST)
    return (maxima, totals, weighted)

def window_attend(query_rows, context_rows, valid_rows):
    level_count, row_count, col_count, channels = query_rows.shape
    head_size = channels // HEADS

    def windows_of(tensor):
        blocks = tensor.reshape(level_count, row_count // WLAT, WLAT, col_count // WLON, WLON, HEADS, head_size)
        blocks = blocks.transpose(1, 3, 0, 2, 4, 5, 6)
        return blocks.reshape(-1, level_count * WLAT * WLON, HEADS, head_size)
    queries = windows_of(query_rows).astype(jnp.float32)
    key_rows = windows_of(context_rows[..., :channels]).astype(jnp.float32)
    value_rows = windows_of(context_rows[..., channels:]).astype(jnp.float32)
    window_mask = jnp.broadcast_to(valid_rows.reshape(row_count // WLAT, 1, 1, WLAT, 1), (row_count // WLAT, col_count // WLON, level_count, WLAT, WLON)).reshape(-1, level_count * WLAT * WLON)
    scores = jnp.einsum('bthc,bshc->bhts', queries, key_rows) * head_size ** (-0.5)
    scores = jnp.where(window_mask[:, None, None, :], scores, masked_score)
    highest = lax.optimization_barrier(jnp.max(scores, axis=-1, keepdims=True))
    weights = jnp.exp(scores - highest)
    shares = (weights / lax.optimization_barrier(jnp.sum(weights, axis=-1, keepdims=True))).astype(jnp.bfloat16)
    attended = jnp.einsum('bhts,bshc->bthc', shares.astype(jnp.float32), value_rows).astype(jnp.bfloat16)
    attended = attended.reshape(row_count // WLAT, col_count // WLON, level_count, WLAT, WLON, channels)
    return attended.transpose(2, 0, 3, 1, 4, 5).reshape(level_count, row_count, col_count, channels)

def reference(patches, level_bias, embed_weight, latent_query, cross_key, cross_value, cross_output, first_gain, window_query, window_context, window_output, second_gain, up_weight, down_weight):
    maxima, totals, weighted = level_partials(patches, level_bias, embed_weight, latent_query, cross_key, cross_value)
    pooled = (weighted / totals[..., None]).astype(jnp.bfloat16).reshape(-1, D)
    latent = jnp.dot(pooled, cross_output, preferred_element_type=jnp.float32).reshape(LATENT, NLAT, NLON, D)
    latent = (latent + latent_query.astype(jnp.float32)[:, None, None, :]).astype(jnp.bfloat16)
    normed = layer_norm(latent.astype(jnp.float32), first_gain).astype(jnp.bfloat16)
    flat_normed = normed.reshape(-1, D)
    query_rows = jnp.dot(flat_normed, window_query, preferred_element_type=jnp.float32).astype(jnp.bfloat16).reshape(LATENT, NLAT, NLON, D)
    context = jnp.dot(flat_normed, window_context, preferred_element_type=jnp.float32).astype(jnp.bfloat16).reshape(LATENT, NLAT, NLON, 2 * D)
    margins = ((0, 0), (SHIFT, SHIFT), (0, 0), (0, 0))
    padded_query = jnp.pad(query_rows, margins)
    padded_context = jnp.pad(context, margins)
    row_ids = jnp.arange(NLAT + WLAT, dtype=jnp.int32)
    valid_rows = (row_ids >= SHIFT) & (row_ids < NLAT + SHIFT)

    def attend_band(window_index):
        begin = (window_index * WLAT).astype(jnp.int32)
        return window_attend(lax.dynamic_slice_in_dim(padded_query, begin, WLAT, 1), lax.dynamic_slice_in_dim(padded_context, begin, WLAT, 1), lax.dynamic_slice_in_dim(valid_rows, begin, WLAT, 0))
    bands = lax.map(attend_band, jnp.arange(NLAT // WLAT + 1, dtype=jnp.int32))
    attended = bands.transpose(1, 0, 2, 3, 4).reshape(LATENT, NLAT + WLAT, NLON, D)[:, SHIFT:SHIFT + NLAT]
    mixed_rows = jnp.dot(attended.reshape(-1, D), window_output, preferred_element_type=jnp.float32) + latent.astype(jnp.float32).reshape(-1, D)
    second = layer_norm(mixed_rows, second_gain).astype(jnp.bfloat16)
    hidden = jax.nn.gelu(jnp.dot(second, up_weight, preferred_element_type=jnp.float32)).astype(jnp.bfloat16)
    result = mixed_rows + jnp.dot(hidden, down_weight, preferred_element_type=jnp.float32)
    return result.reshape(LATENT, NLAT, NLON, D).astype(jnp.bfloat16)
```

```python
import functools

import jax
import jax.numpy as jnp
from jax import lax
from jax.experimental import pallas as pl
from jax.experimental.pallas import tpu as pltpu
from jax.sharding import PartitionSpec as P

HEADS = 16
HEAD = 32
D = 512
LATENT = 3
LEVELS = 8
ROWS = 6
COLS = 12
PIXELS = 80
SHIFT = 3
WIDE = 1024
HALF = 112
FILLED = 108
TOKENS = 2 * HALF
FOLDED = 768
EPSILON = 1e-05
MASKED = -1e30
SCALE = HEAD**-0.5
F32 = jnp.float32
BF16 = jnp.bfloat16


def dot(a, b):
    return jnp.dot(a, b, preferred_element_type=F32)


def dot_nt(a, b):
    return lax.dot_general(a, b, (((1,), (1,)), ((), ())), preferred_element_type=F32)


def split(a):
    high = a.astype(BF16)
    return high, (a - high.astype(F32)).astype(BF16)


def iota(shape, dim):
    return lax.broadcasted_iota(jnp.int32, shape, dim)


def layer_norm(tensor, scales):
    center = jnp.mean(tensor, axis=-1, keepdims=True)
    offset = tensor - center
    spread = jnp.mean(offset * offset, axis=-1, keepdims=True)
    return offset * lax.rsqrt(spread + EPSILON) * scales


def blocks_kernel(pixels, out):
    out[...] = jnp.zeros_like(out)
    wide = pixels[0].astype(F32)
    for v in range(8):
        out[v, :ROWS, : COLS * PIXELS] = wide[:, v * COLS * PIXELS : (v + 1) * COLS * PIXELS].astype(BF16)


def fold_kernel(bias, embed, query, key, value, folded, folded_bias):
    head_of_lane = iota((HEADS, D), 1) // HEAD
    own = head_of_lane == iota((HEADS, D), 0)
    spread = [jnp.where(own, query[q : q + 1].astype(F32), 0.0) for q in range(LATENT)]
    spread.append(jnp.zeros((128 - LATENT * HEADS, D), F32))
    spread = jnp.concatenate(spread, axis=0).astype(BF16)
    high, low = split(dot_nt(key[...], spread))
    scores = dot(embed[...], high) + dot(embed[...], low)
    high_score, low_score = split(scores)
    values = dot(embed[...], value[...]).astype(BF16)
    whole = jnp.concatenate([values, high_score, low_score], axis=1)
    folded[...] = jnp.zeros_like(folded)
    for k in range(8):
        folded[k, 16 * k : 16 * k + PIXELS] = whole
    folded_bias[:, :D] = dot(bias[...], value[...])
    folded_bias[:, D:] = dot(bias[...], high) + dot(bias[...], low)


def pool_rows(x, folded, folded_bias, values, weights, pooled):
    bias_value = folded_bias[:, :D][:, None, :]
    bias_score = folded_bias[:, D:][:, None, :]
    for j in range(COLS):
        start, offset = j * PIXELS // 128 * 128, j * PIXELS % 128
        got = dot(x[:, start : start + 256], folded[offset // 16])
        values[j] = got[:, :D].reshape(LEVELS, 8, D) + bias_value
        score = (got[:, D : D + 128] + got[:, D + 128 :]).reshape(LEVELS, 8, 128) + bias_score
        share = jnp.exp((score - jnp.max(score, axis=0, keepdims=True)) * SCALE)
        share = share / jnp.sum(share, axis=0, keepdims=True)
        high, low = split(share.reshape(64, 128))
        weights[j * 64 : (j + 1) * 64, :128] = high
        weights[j * 64 : (j + 1) * 64, 128:] = low
    for q in range(LATENT):
        lane = (iota((256, D), 1) >> 5) + q * HEADS
        expand = jnp.where((iota((256, D), 0) & 127) == lane, 1.0, 0.0).astype(BF16)
        full = dot(weights[...], expand).reshape(COLS, LEVELS, 8, D)
        total = jnp.sum(full * values[...], axis=1)
        pooled[q * 96 : (q + 1) * 96] = total.reshape(96, D).astype(BF16)
    source = iota((1, 288), 1)
    q = (source >= 96).astype(jnp.int32) + (source >= 192).astype(jnp.int32)
    j = (source - 96 * q) >> 3
    row = source & 7
    half = (row >= 3).astype(jnp.int32)
    target = half * HALF + (q * 3 + row - 3 * half) * 12 + j
    target = jnp.where(row < ROWS, target, -1)
    pick = jnp.where(iota((TOKENS, 288), 0) == target, 1.0, 0.0).astype(BF16)
    return dot(pick, pooled[...]).astype(BF16)


def latent_rows(pooled, query, output):
    place = iota((TOKENS, 1), 0)
    place = jnp.where(place >= HALF, place - HALF, place)
    first, second, third = (query[q : q + 1].astype(F32) for q in range(LATENT))
    added = jnp.where(place < 36, first, jnp.where(place < 72, second, third))
    return (dot(pooled, output[...]) + added).astype(BF16)


def own_kernel(x, folded, folded_bias, query, output, gain, to_query, to_context,
               latent, spread_query, context, values, weights, pooled):
    rows = pool_rows(x[...].reshape(64, WIDE), folded, folded_bias, values, weights, pooled)
    tokens = latent_rows(rows, query, output)
    latent[...] = tokens
    normed = layer_norm(tokens.astype(F32), gain[...]).astype(BF16)
    queries = dot(normed, to_query[...]).astype(BF16).astype(F32)
    context[...] = dot(normed, to_context[...]).astype(BF16)
    spread_query[...] = jnp.zeros_like(spread_query)
    for half in range(2):
        part = queries[half * HALF : (half + 1) * HALF]
        part = jnp.concatenate([part, jnp.zeros((128 - HALF, D), F32)], axis=0)
        turned = part.T.astype(BF16)
        for head in range(HEADS):
            group, place = divmod(head, 8)
            spread_query[half * 2 + group, place * HEAD : (place + 1) * HEAD, place * 128 : (place + 1) * 128] = (
                turned[head * HEAD : (head + 1) * HEAD]
            )


def block_kernel(bands, x, folded, folded_bias, query, output, gain, to_context, latent, spread_query, context,
                 mix, second_gain, up, down, out, values, weights, pooled):
    rows = pool_rows(x[...].reshape(64, WIDE), folded, folded_bias, values, weights, pooled)
    tokens = latent_rows(rows, query, output)
    normed = layer_norm(tokens.astype(F32), gain[...]).astype(BF16)
    beside = dot(normed, to_context[...]).astype(BF16)
    band = lax.axis_index("lat")
    place = iota((TOKENS, 1), 0)
    filled = jnp.where(place >= HALF, place - HALF, place) < FILLED
    mixed = []
    for half in range(2):
        own = context[half * HALF : (half + 1) * HALF]
        near = jnp.concatenate([own, beside[half * HALF : (half + 1) * HALF]], axis=0)
        there = band > 0 if half == 0 else band < bands - 1
        usable = filled & ((place < HALF) | there)
        mask = jnp.where(usable, 0.0, MASKED)
        parts = []
        for group in range(2):
            keys = near[:, group * 256 : (group + 1) * 256]
            score = dot(keys, spread_query[half * 2 + group]) + mask
            share = jnp.exp((score - jnp.max(score, axis=0, keepdims=True)) * SCALE)
            inverse = 1.0 / jnp.sum(share, axis=0, keepdims=True)
            share = share.astype(BF16)
            turned = near[:, D + group * 256 : D + (group + 1) * 256].astype(F32).T.astype(BF16)
            for head in range(8):
                lanes = slice(head * 128, (head + 1) * 128)
                part = dot(turned[head * HEAD : (head + 1) * HEAD], share[:, lanes])
                parts.append(part * inverse[:, lanes])
        attended = jnp.concatenate(parts, axis=0).T.astype(BF16)
        mixed.append(dot(attended, mix[...])[:HALF])
    mixed = jnp.concatenate(mixed, axis=0) + latent[...].astype(F32)
    second = layer_norm(mixed, second_gain[...]).astype(BF16)
    hidden = jax.nn.gelu(dot(second, up[...])).astype(BF16)
    result = mixed + dot(hidden, down[...])
    for half in range(2):
        for q in range(LATENT):
            for i in range(3):
                start = half * HALF + (q * 3 + i) * COLS
                out[q, half * 3 + i] = result[start : start + COLS].astype(BF16)


def call(kernel, outs, scratch=(), flops=0, moved=0, limit=32):
    return pl.pallas_call(
        kernel,
        out_shape=outs,
        scratch_shapes=list(scratch),
        compiler_params=pltpu.CompilerParams(vmem_limit_bytes=limit * 2**20),
        cost_estimate=pl.CostEstimate(flops=flops, bytes_accessed=moved, transcendentals=0),
    )


def shaped(*shape, dtype=BF16):
    return jax.ShapeDtypeStruct(shape, dtype)


def body(
    patches,
    level_bias,
    embed_weight,
    latent_query,
    cross_key,
    cross_value,
    cross_output,
    first_gain,
    window_query,
    window_context,
    window_output,
    second_gain,
    up_weight,
    down_weight,
):
    bands = lax.axis_size("lat")
    blocks = call(blocks_kernel, shaped(8, 8, WIDE), flops=10**6, moved=10**6)(patches)
    x = lax.all_to_all(blocks, "var", 0, 0, tiled=True)
    folded, folded_bias = call(
        fold_kernel,
        (shaped(8, 256, FOLDED), shaped(LEVELS, D + 128, dtype=F32)),
        flops=10**9,
        moved=6 * 10**6,
    )(level_bias, embed_weight, latent_query, cross_key, cross_value)
    forward = [(i, i + 1) for i in range(bands - 1)]
    backward = [(i + 1, i) for i in range(bands - 1)]
    low = lax.ppermute(x[:, SHIFT:ROWS], "lat", forward)
    high = lax.ppermute(x[:, :SHIFT], "lat", backward)
    scratch = (
        pltpu.VMEM((COLS, LEVELS, 8, D), F32),
        pltpu.VMEM((COLS * 64, 256), BF16),
        pltpu.VMEM((LATENT * 96, D), BF16),
    )
    gain = first_gain.reshape(1, D)
    latent, spread_query, context = call(
        own_kernel,
        (shaped(TOKENS, D), shaped(4, 256, 1024), shaped(TOKENS, 2 * D)),
        scratch,
        flops=3 * 10**9,
        moved=10**7,
    )(x, folded, folded_bias, latent_query, cross_output, gain, window_query, window_context)
    beside = jnp.concatenate([low, high, jnp.zeros((LEVELS, 2, WIDE), BF16)], axis=1)
    return call(
        functools.partial(block_kernel, bands),
        shaped(LATENT, ROWS, COLS, D),
        scratch,
        flops=4 * 10**9,
        moved=10**7,
    )(beside, folded, folded_bias, latent_query, cross_output, gain, window_context, latent, spread_query, context,
      window_output, second_gain.reshape(1, D), up_weight, down_weight)


def solution(mesh):
    return jax.shard_map(
        body,
        mesh=mesh,
        in_specs=(P(("dp", "var"), "lat", None),) + (P(),) * 13,
        out_specs=P("dp", "lat", "var", None),
        check_vma=False,
    )
```

```python
import functools

import jax
import jax.numpy as jnp
from jax import lax
from jax.experimental import pallas as pl
from jax.experimental.pallas import tpu as pltpu
from jax.sharding import Mesh
from jax.sharding import PartitionSpec as P

HEADS = 16
HEAD = 32
D = 512
LATENT = 3
LEVELS = 8
ROWS = 6
COLS = 12
PIXELS = 80
WIDE = 1024
HALF = 112
FILLED = 108
TOKENS = 2 * HALF
FOLDED = 768
EPSILON = 1e-05
MASKED = -1e30
SCALE = HEAD**-0.5
F32 = jnp.float32
BF16 = jnp.bfloat16


def dot(a, b):
    return jnp.dot(a, b, preferred_element_type=F32)


def dot_nt(a, b):
    return lax.dot_general(a, b, (((1,), (1,)), ((), ())), preferred_element_type=F32)


def split(a):
    high = a.astype(BF16)
    return high, (a - high.astype(F32)).astype(BF16)


def iota(shape, dim):
    return lax.broadcasted_iota(jnp.int32, shape, dim)


def layer_norm(tensor, scales):
    center = jnp.mean(tensor, axis=-1, keepdims=True)
    offset = tensor - center
    spread = jnp.mean(offset * offset, axis=-1, keepdims=True)
    return offset * lax.rsqrt(spread + EPSILON) * scales


def blocks_kernel(pixels, out, held, arrived):
    copy = pltpu.make_async_copy(pixels, held, arrived)
    copy.start()
    out[...] = jnp.zeros_like(out)
    copy.wait()
    wide = held[0].astype(F32)
    for v in range(LEVELS):
        block = wide[:, v * COLS * PIXELS : (v + 1) * COLS * PIXELS].astype(BF16)
        out[2 * v, :ROWS, : COLS * PIXELS] = block
        out[2 * v + 1, :ROWS, : COLS * PIXELS] = block


def pick_matrix(swapped):
    source = iota((1, 288), 1)
    q = (source >= 96).astype(jnp.int32) + (source >= 192).astype(jnp.int32)
    j = (source - 96 * q) >> 3
    row = source & 7
    lower = (row >= 3).astype(jnp.int32)
    half = 1 - lower if swapped else lower
    target = half * HALF + (q * 3 + row - 3 * lower) * COLS + j
    target = jnp.where(row < ROWS, target, -1)
    return jnp.where(iota((TOKENS, 288), 0) == target, 1.0, 0.0).astype(BF16)


def fold_kernel(bias_hbm, embed_hbm, query_hbm, key_hbm, value_hbm, folded, folded_bias, expand,
                bias, embed, query, key, value, arrived):
    pairs = ((query_hbm, query), (key_hbm, key), (embed_hbm, embed), (value_hbm, value), (bias_hbm, bias))
    copies = [pltpu.make_async_copy(*pair, arrived.at[k]) for k, pair in enumerate(pairs)]
    for copy in copies:
        copy.start()
    for q in range(LATENT):
        lane = (iota((256, D), 1) >> 5) + q * HEADS
        expand[:, q * D : (q + 1) * D] = jnp.where((iota((256, D), 0) & 127) == lane, 1.0, 0.0).astype(BF16)
    for copy in copies:
        copy.wait()
    own = iota((HEADS, D), 1) // HEAD == iota((HEADS, D), 0)
    spread = [jnp.where(own, query[q : q + 1].astype(F32), 0.0) for q in range(LATENT)]
    spread.append(jnp.zeros((128 - LATENT * HEADS, D), F32))
    spread = jnp.concatenate(spread, axis=0).astype(BF16)
    high, low = split(dot_nt(key[...], spread))
    scores = dot(embed[...], high) + dot(embed[...], low)
    high_score, low_score = split(scores)
    folded[PIXELS:] = jnp.zeros((128 - PIXELS, FOLDED), BF16)
    folded[:PIXELS, :D] = dot(embed[...], value[...]).astype(BF16)
    folded[:PIXELS, D : D + 128] = high_score
    folded[:PIXELS, D + 128 :] = low_score
    folded_bias[:, :D] = dot(bias[...], value[...])
    folded_bias[:, D:] = dot(bias[...], high) + dot(bias[...], low)


def pool_rows(x, folded, folded_bias, expand, query, output, swapped, rows, values, weights, pooled):
    for j in range(COLS):
        rows[j * 64 : (j + 1) * 64] = x[:, j * PIXELS : j * PIXELS + 128].astype(BF16)
    values[...] = dot(rows[...], folded[:, :D]).reshape(COLS, LEVELS, 8, D) + folded_bias[:, :D][None, :, None, :]
    both = dot(rows[...], folded[:, D:])
    score = (both[:, :128] + both[:, 128:]).reshape(COLS, LEVELS, 8, 128) + folded_bias[:, D:][None, :, None, :]
    share = jnp.exp((score - jnp.max(score, axis=1, keepdims=True)) * SCALE)
    share = share / jnp.sum(share, axis=1, keepdims=True)
    high, low = split(share.reshape(COLS * 64, 128))
    weights[:, :128] = high
    weights[:, 128:] = low
    for q in range(LATENT):
        full = dot(weights[...], expand[:, q * D : (q + 1) * D]).reshape(COLS, LEVELS, 8, D)
        total = jnp.sum(full * values[...], axis=1)
        pooled[q * 96 : (q + 1) * 96] = total.reshape(96, D).astype(BF16)
    picked = dot(pick_matrix(swapped), pooled[...]).astype(BF16)
    place = iota((TOKENS, 1), 0)
    place = jnp.where(place >= HALF, place - HALF, place)
    first, second, third = (query[q : q + 1].astype(F32) for q in range(LATENT))
    added = jnp.where(place < 36, first, jnp.where(place < 72, second, third))
    return (dot(picked, output[...]) + added).astype(BF16)


def own_kernel(x, folded, folded_bias, expand, query, output, gain, to_query, to_context,
               latent, spread_query, context, *scratch):
    own = x[:, pl.ds(lax.axis_index("near"), 1)].reshape(64, WIDE).astype(F32)
    tokens = pool_rows(own, folded, folded_bias, expand, query, output, False, *scratch)
    latent[...] = tokens
    normed = layer_norm(tokens.astype(F32), gain[...]).astype(BF16)
    queries = dot(normed, to_query[...]).astype(BF16).astype(F32)
    context[...] = dot(normed, to_context[...]).astype(BF16)
    spread_query[...] = jnp.zeros_like(spread_query)
    for half in range(2):
        part = queries[half * HALF : (half + 1) * HALF]
        part = jnp.concatenate([part, jnp.zeros((128 - HALF, D), F32)], axis=0)
        turned = part.T.astype(BF16)
        for head in range(HEADS):
            group, place = divmod(head, 8)
            spread_query[half * 2 + group, place * HEAD : (place + 1) * HEAD, place * 128 : (place + 1) * 128] = (
                turned[head * HEAD : (head + 1) * HEAD]
            )


def block_kernel(pairs, x, beyond, folded, folded_bias, expand, query, output, gain, to_context,
                 latent, spread_query, context, mix, second_gain, up, down, out, *scratch):
    near = lax.axis_index("near")
    inner = x[:, pl.ds(1 - near, 1)].reshape(64, WIDE).astype(F32)
    lower = (iota((64, 1), 0) & 7) >= 3
    halo = jnp.where(lower == (near == 1), inner, beyond[...].reshape(64, WIDE).astype(F32))
    tokens = pool_rows(halo, folded, folded_bias, expand, query, output, True, *scratch)
    normed = layer_norm(tokens.astype(F32), gain[...]).astype(BF16)
    beside = dot(normed, to_context[...]).astype(BF16)
    band = lax.axis_index("far") * 2 + near
    place = iota((TOKENS, 1), 0)
    filled = jnp.where(place >= HALF, place - HALF, place) < FILLED
    mixed = []
    for half in range(2):
        own = context[half * HALF : (half + 1) * HALF]
        keys = jnp.concatenate([own, beside[half * HALF : (half + 1) * HALF]], axis=0)
        there = band > 0 if half == 0 else band < 2 * pairs - 1
        usable = filled & ((place < HALF) | there)
        mask = jnp.where(usable, 0.0, MASKED)
        parts = []
        for group in range(2):
            score = dot(keys[:, group * 256 : (group + 1) * 256], spread_query[half * 2 + group]) + mask
            share = jnp.exp((score - jnp.max(score, axis=0, keepdims=True)) * SCALE)
            inverse = 1.0 / jnp.sum(share, axis=0, keepdims=True)
            share = share.astype(BF16)
            turned = keys[:, D + group * 256 : D + (group + 1) * 256].astype(F32).T.astype(BF16)
            for head in range(8):
                lanes = slice(head * 128, (head + 1) * 128)
                part = dot(turned[head * HEAD : (head + 1) * HEAD], share[:, lanes])
                parts.append(part * inverse[:, lanes])
        attended = jnp.concatenate(parts, axis=0).T.astype(BF16)
        mixed.append(dot(attended, mix[...])[:HALF])
    mixed = jnp.concatenate(mixed, axis=0) + latent[...].astype(F32)
    second = layer_norm(mixed, second_gain[...]).astype(BF16)
    hidden = jax.nn.gelu(dot(second, up[...])).astype(BF16)
    result = mixed + dot(hidden, down[...])
    for half in range(2):
        for q in range(LATENT):
            for i in range(3):
                start = half * HALF + (q * 3 + i) * COLS
                out[q, half * 3 + i] = result[start : start + COLS].astype(BF16)


def call(kernel, outs, scratch=(), flops=0, moved=0, limit=24, hbm=0):
    specs = {"in_specs": [pl.BlockSpec(memory_space=pltpu.HBM)] * hbm} if hbm else {}
    return pl.pallas_call(
        kernel,
        out_shape=outs,
        scratch_shapes=list(scratch),
        compiler_params=pltpu.CompilerParams(vmem_limit_bytes=limit * 2**20),
        cost_estimate=pl.CostEstimate(flops=flops, bytes_accessed=moved, transcendentals=0),
        **specs,
    )


def shaped(*shape, dtype=BF16):
    return jax.ShapeDtypeStruct(shape, dtype)


def body(
    patches,
    level_bias,
    embed_weight,
    latent_query,
    cross_key,
    cross_value,
    cross_output,
    first_gain,
    window_query,
    window_context,
    window_output,
    second_gain,
    up_weight,
    down_weight,
):
    pairs = lax.axis_size("far")
    blocks = call(
        blocks_kernel,
        shaped(2 * LEVELS, 8, WIDE),
        (pltpu.VMEM(patches.shape, BF16), pltpu.SemaphoreType.DMA),
        flops=10**6,
        moved=10**6,
        hbm=1,
    )(pltpu.with_memory_space_constraint(patches, pltpu.HBM))
    x = lax.all_to_all(blocks, ("var", "near"), 0, 0, tiled=True).reshape(LEVELS, 2, 8, WIDE)
    folded, folded_bias, expand = call(
        fold_kernel,
        (
            shaped(128, FOLDED),
            shaped(LEVELS, D + 128, dtype=F32),
            shaped(256, LATENT * D),
        ),
        tuple(pltpu.VMEM(a.shape, BF16) for a in (level_bias, embed_weight, latent_query, cross_key, cross_value))
        + (pltpu.SemaphoreType.DMA((5,)),),
        flops=10**9,
        moved=6 * 10**6,
        hbm=5,
    )(
        *(
            pltpu.with_memory_space_constraint(a, pltpu.HBM)
            for a in (level_bias, embed_weight, latent_query, cross_key, cross_value)
        )
    )
    swaps = [(2 * k + 1, 2 * k + 2) for k in range(pairs - 1)]
    swaps += [(b, a) for a, b in swaps]
    mine = lax.dynamic_index_in_dim(x, lax.axis_index("near"), 1, keepdims=False)
    beyond = lax.ppermute(mine, ("far", "near"), swaps)
    scratch = (
        pltpu.VMEM((COLS * 64, 128), BF16),
        pltpu.VMEM((COLS, LEVELS, 8, D), F32),
        pltpu.VMEM((COLS * 64, 256), BF16),
        pltpu.VMEM((LATENT * 96, D), BF16),
    )
    gain = first_gain.reshape(1, D)
    latent, spread_query, context = call(
        own_kernel,
        (shaped(TOKENS, D), shaped(4, 256, 1024), shaped(TOKENS, 2 * D)),
        scratch,
        flops=3 * 10**9,
        moved=10**7,
    )(x, folded, folded_bias, expand, latent_query, cross_output, gain, window_query, window_context)
    return call(
        functools.partial(block_kernel, pairs),
        shaped(LATENT, ROWS, COLS, D),
        scratch,
        flops=4 * 10**9,
        moved=10**7,
    )(x, beyond, folded, folded_bias, expand, latent_query, cross_output, gain, window_context, latent,
      spread_query, context, window_output, second_gain.reshape(1, D), up_weight, down_weight)


def solution(mesh):
    finer = Mesh(
        mesh.devices.reshape(mesh.shape["var"], mesh.shape["lat"] // 2, 2, mesh.shape["dp"]),
        ("var", "far", "near", "dp"),
    )
    return jax.shard_map(
        body,
        mesh=finer,
        in_specs=(P(("dp", "var"), ("far", "near"), None),) + (P(),) * 13,
        out_specs=P("dp", ("far", "near"), "var", None),
        check_vma=False,
    )
```

```python
import functools
import math

import jax
import jax.numpy as jnp
from jax import lax
from jax.experimental import pallas as pl
from jax.experimental.pallas import tpu as pltpu
from jax.sharding import Mesh
from jax.sharding import PartitionSpec as P

HEADS = 16
HEAD = 32
D = 512
LATENT = 3
LEVELS = 8
ROWS = 6
COLS = 12
PIXELS = 80
WIDE = 1024
HALF = 112
FILLED = 108
TOKENS = 2 * HALF
FOLDED = 768
EPSILON = 1e-05
HALO_TILES = 6
TILES = 9
RATE = HEAD**-0.5 * math.log2(math.e)
F32 = jnp.float32
BF16 = jnp.bfloat16


def dot(a, b):
    return jnp.dot(a, b, preferred_element_type=F32)


def dot_nt(a, b):
    return lax.dot_general(a, b, (((1,), (1,)), ((), ())), preferred_element_type=F32)


def split(a):
    high = a.astype(BF16)
    return high, (a - high.astype(F32)).astype(BF16)


def iota(shape, dim):
    return lax.broadcasted_iota(jnp.int32, shape, dim)


def layer_norm(tensor, scales):
    center = jnp.mean(tensor, axis=-1, keepdims=True)
    offset = tensor - center
    spread = jnp.mean(offset * offset, axis=-1, keepdims=True)
    return offset * lax.rsqrt(spread + EPSILON) * scales


def blocks_kernel(pixels, out, held, arrived):
    copy = pltpu.make_async_copy(pixels, held, arrived)
    copy.start()
    out[...] = jnp.zeros_like(out)
    copy.wait()
    wide = held[0].astype(F32)
    for v in range(LEVELS):
        block = wide[:, v * COLS * PIXELS : (v + 1) * COLS * PIXELS].astype(BF16)
        out[2 * v, :ROWS, : COLS * PIXELS] = block
        out[2 * v + 1, :ROWS, : COLS * PIXELS] = block


def fold_kernel(bias_hbm, embed_hbm, query_hbm, key_hbm, value_hbm, folded, folded_bias, expand,
                bias, embed, query, key, value, arrived):
    pairs = ((query_hbm, query), (key_hbm, key), (embed_hbm, embed), (value_hbm, value), (bias_hbm, bias))
    copies = [pltpu.make_async_copy(*pair, arrived.at[k]) for k, pair in enumerate(pairs)]
    for copy in copies:
        copy.start()
    for q in range(LATENT):
        lane = (iota((256, D), 1) >> 5) + q * HEADS
        expand[:, q * D : (q + 1) * D] = jnp.where((iota((256, D), 0) & 127) == lane, 1.0, 0.0).astype(BF16)
    for copy in copies:
        copy.wait()
    own = iota((HEADS, D), 1) // HEAD == iota((HEADS, D), 0)
    spread = [jnp.where(own, query[q : q + 1].astype(F32), 0.0) for q in range(LATENT)]
    spread.append(jnp.zeros((128 - LATENT * HEADS, D), F32))
    spread = jnp.concatenate(spread, axis=0).astype(BF16)
    high, low = split(dot_nt(key[...], spread))
    scores = dot(embed[...], high) + dot(embed[...], low)
    high_score, low_score = split(scores)
    folded[PIXELS:] = jnp.zeros((128 - PIXELS, FOLDED), BF16)
    folded[:PIXELS, :D] = dot(embed[...], value[...]).astype(BF16)
    folded[:PIXELS, D : D + 128] = high_score
    folded[:PIXELS, D + 128 :] = low_score
    folded_bias[:, :D] = dot(bias[...], value[...])
    folded_bias[:, D:] = dot(bias[...], high) + dot(bias[...], low)


def pick_own(near):
    source = iota((1, LATENT * TILES * 8), 1)
    q = (source >= TILES * 8).astype(jnp.int32) + (source >= 2 * TILES * 8).astype(jnp.int32)
    source = source - TILES * 8 * q
    tile, place = source >> 3, source & 7
    group = (tile >= 3).astype(jnp.int32) + (tile >= 6).astype(jnp.int32)
    member = tile - 3 * group
    j = 4 * group + jnp.where(place < ROWS, member, 3)
    row = jnp.where(place < ROWS, place, 2 * member + place - ROWS)
    lower = (row >= 3).astype(jnp.int32)
    half = jnp.where(lower == near, 1, 0)
    source = half * HALF + (q * 3 + row - 3 * lower) * COLS + j
    target = iota((TOKENS, 1), 0)
    spare = jnp.where(target >= HALF, target - HALF, target) >= FILLED
    target = jnp.where(spare, target - (HALF - FILLED), target)
    return jnp.where(source == target, 1.0, 0.0).astype(BF16)


def pick_halo():
    source = iota((1, LATENT * HALO_TILES * 8), 1)
    q = (source >= HALO_TILES * 8).astype(jnp.int32) + (source >= 2 * HALO_TILES * 8).astype(jnp.int32)
    source = source - HALO_TILES * 8 * q
    tile, place = source >> 3, source & 7
    second = (place >= 3).astype(jnp.int32)
    source = jnp.where(place < 6, (q * 3 + place - 3 * second) * COLS + 2 * tile + second, -1)
    target = iota((HALF, 1), 0)
    target = jnp.where(target >= FILLED, target - (HALF - FILLED), target)
    return jnp.where(source == target, 1.0, 0.0).astype(BF16)


def patches_of(x, first, last):
    return [x[:, :, j * PIXELS : j * PIXELS + 128] for j in range(first, last)]


def own_rows(x, rows):
    full = iota((LEVELS, 8, 128), 1) < ROWS
    for group in range(3):
        four = patches_of(x, 4 * group, 4 * group + 4)
        for member in range(3):
            tile = jnp.where(full, four[member], pltpu.roll(four[3], ROWS - 2 * member, 1))
            start = (group * 3 + member) * 64
            rows[start : start + 64] = tile.reshape(64, 128).astype(BF16)


def halo_rows(x, lower, rows):
    x = jnp.where(lower, pltpu.roll(x, 5, 1), x)
    first = iota((LEVELS, 8, 128), 1) < 3
    for pair in range(HALO_TILES):
        left, right = patches_of(x, 2 * pair, 2 * pair + 2)
        tile = jnp.where(first, left, pltpu.roll(right, 3, 1))
        rows[pair * 64 : (pair + 1) * 64] = tile.reshape(64, 128).astype(BF16)


def pool(folded, folded_bias, expand, rows, values, weights, pooled):
    tiles = rows.shape[0] // 64
    both = dot(rows[...], folded[:, D:])
    score = (both[:, :128] + both[:, 128:]).reshape(tiles, LEVELS, 8, 128) + folded_bias[:, D:][None, :, None, :]
    share = jnp.exp2((score - jnp.max(score, axis=1, keepdims=True)) * RATE)
    share = share / jnp.sum(share, axis=1, keepdims=True)
    high, low = split(share.reshape(tiles * 64, 128))
    weights[:, :128] = high
    weights[:, 128:] = low
    values[...] = dot(rows[...], folded[:, :D]).reshape(tiles, LEVELS, 8, D) + folded_bias[:, :D][None, :, None, :]
    for q in range(LATENT):
        full = dot(weights[...], expand[:, q * D : (q + 1) * D]).reshape(tiles, LEVELS, 8, D)
        total = jnp.sum(full * values[...], axis=1).astype(BF16)
        start = 0
        for array in pooled:
            size = array.shape[0] // LATENT
            array[q * size : (q + 1) * size] = total[start : start + size // 8].reshape(size, D)
            start += size // 8


def latent_rows(picked, query, output):
    place = iota((HALF, 1), 0)
    first, second, third = (query[q : q + 1].astype(F32) for q in range(LATENT))
    added = jnp.where(place < 36, first, jnp.where(place < 72, second, third))
    added = jnp.concatenate([added] * (picked.shape[0] // HALF), axis=0)
    return (dot(picked.astype(BF16), output[...]) + added).astype(BF16)


def spread_heads(queries, spread):
    part = jnp.concatenate([queries, jnp.zeros((128 - HALF, D), F32)], axis=0).T.astype(BF16)
    spread[...] = jnp.zeros_like(spread)
    for head in range(HEADS):
        group, spot = divmod(head, 4)
        spread[group, spot * HEAD : (spot + 1) * HEAD, spot * 128 : (spot + 1) * 128] = (
            part[head * HEAD : (head + 1) * HEAD]
        )


def attend(spread, own, beside, there):
    lane = iota((1, TOKENS), 1)
    filled = jnp.where(lane >= HALF, lane - HALF, lane) < FILLED
    usable = jnp.where(filled & ((lane < HALF) | there), 1.0, 0.0)
    keys = jnp.concatenate([own[:, :D], jnp.where(there, beside[:, :D], own[:, :D])], axis=0)
    turned = jnp.concatenate([own[:, D:], beside[:, D:]], axis=0).astype(F32).T
    turned = jnp.where(usable > 0.0, turned, 0.0).astype(BF16)
    count = jnp.broadcast_to(usable, (16, TOKENS)).astype(BF16)
    parts = []
    for group in range(4):
        score = dot(keys[:, group * 128 : (group + 1) * 128], spread[group])
        share = jnp.exp2((score - jnp.max(score, axis=0, keepdims=True)) * RATE).astype(BF16)
        for pair in range(2):
            start = (group * 2 + pair) * 2 * HEAD
            weighed = jnp.concatenate([turned[start : start + 2 * HEAD], count], axis=0)
            got = dot(weighed, share[:, pair * 256 : (pair + 1) * 256])
            inverse = 1.0 / got[2 * HEAD : 2 * HEAD + 1]
            parts.append(got[:HEAD, :128] * inverse[:, :128])
            parts.append(got[HEAD : 2 * HEAD, 128:] * inverse[:, 128:])
    return jnp.concatenate(parts, axis=0).T[:HALF].astype(BF16)


def own_kernel(x, folded, folded_bias, expand, query, output, gain, to_query, to_context,
               latent, attended, spread_query, context, rows, values, weights, pooled, halo_pooled, spread_here):
    near = lax.axis_index("near")
    own_rows(x[:, pl.ds(near, 1)].reshape(LEVELS, 8, WIDE).astype(F32), rows.at[: TILES * 64])
    halo_rows(x[:, pl.ds(1 - near, 1)].reshape(LEVELS, 8, WIDE).astype(F32), near == 1, rows.at[TILES * 64 :])
    pool(folded, folded_bias, expand, rows, values, weights, (pooled, halo_pooled))
    picked = jnp.concatenate([dot(pick_own(near), pooled[...]), dot(pick_halo(), halo_pooled[...])], axis=0)
    tokens = latent_rows(picked, query, output)
    latent[...] = tokens[:TOKENS]
    normed = layer_norm(tokens.astype(F32), gain[...]).astype(BF16)
    queries = dot(normed[:TOKENS], to_query[...]).astype(BF16).astype(F32)
    seen = dot(normed, to_context[...]).astype(BF16)
    context[...] = seen[HALF:TOKENS]
    spread_heads(queries[HALF:], spread_query)
    spread_heads(queries[:HALF], spread_here)
    attended[...] = attend(spread_here, seen[:HALF], seen[TOKENS:], True)


def block_kernel(pairs, beyond, folded, folded_bias, expand, query, output, gain, to_context, latent, attended,
                 spread_query, context, mix, second_gain, up, down, out, rows, values, weights, halo_pooled):
    near = lax.axis_index("near")
    band = lax.axis_index("far") * 2 + near
    halo_rows(beyond[...].astype(F32), near == 0, rows)
    pool(folded, folded_bias, expand, rows, values, weights, (halo_pooled,))
    tokens = latent_rows(dot(pick_halo(), halo_pooled[...]), query, output)
    normed = layer_norm(tokens.astype(F32), gain[...]).astype(BF16)
    beside = dot(normed, to_context[...]).astype(BF16)
    there = (band > 0) & (band < 2 * pairs - 1)
    second_half = attend(spread_query, context[...], beside, there)
    both = jnp.concatenate([attended[...], second_half], axis=0)
    mixed = dot(both, mix[...]) + latent[...].astype(F32)
    second = layer_norm(mixed, second_gain[...]).astype(BF16)
    hidden = jax.nn.gelu(dot(second, up[...])).astype(BF16)
    result = mixed + dot(hidden, down[...])
    for half in range(2):
        first_row = (1 - near if half == 0 else near) * 3
        for q in range(LATENT):
            for i in range(3):
                start = half * HALF + (q * 3 + i) * COLS
                out[q, pl.ds(first_row + i, 1)] = result[start : start + COLS].astype(BF16)[None]


def call(kernel, outs, scratch=(), flops=0, moved=0, limit=24, hbm=0):
    specs = {"in_specs": [pl.BlockSpec(memory_space=pltpu.HBM)] * hbm} if hbm else {}
    return pl.pallas_call(
        kernel,
        out_shape=outs,
        scratch_shapes=list(scratch),
        compiler_params=pltpu.CompilerParams(vmem_limit_bytes=limit * 2**20),
        cost_estimate=pl.CostEstimate(flops=flops, bytes_accessed=moved, transcendentals=0),
        **specs,
    )


def shaped(*shape, dtype=BF16):
    return jax.ShapeDtypeStruct(shape, dtype)


def body(
    patches,
    level_bias,
    embed_weight,
    latent_query,
    cross_key,
    cross_value,
    cross_output,
    first_gain,
    window_query,
    window_context,
    window_output,
    second_gain,
    up_weight,
    down_weight,
):
    pairs = lax.axis_size("far")
    blocks = call(
        blocks_kernel,
        shaped(2 * LEVELS, 8, WIDE),
        (pltpu.VMEM(patches.shape, BF16), pltpu.SemaphoreType.DMA),
        flops=10**6,
        moved=10**6,
        hbm=1,
    )(pltpu.with_memory_space_constraint(patches, pltpu.HBM))
    x = lax.all_to_all(blocks, ("var", "near"), 0, 0, tiled=True).reshape(LEVELS, 2, 8, WIDE)
    folded, folded_bias, expand = call(
        fold_kernel,
        (
            shaped(128, FOLDED),
            shaped(LEVELS, D + 128, dtype=F32),
            shaped(256, LATENT * D),
        ),
        tuple(pltpu.VMEM(a.shape, BF16) for a in (level_bias, embed_weight, latent_query, cross_key, cross_value))
        + (pltpu.SemaphoreType.DMA((5,)),),
        flops=10**9,
        moved=6 * 10**6,
        hbm=5,
    )(
        *(
            pltpu.with_memory_space_constraint(a, pltpu.HBM)
            for a in (level_bias, embed_weight, latent_query, cross_key, cross_value)
        )
    )
    swaps = [(2 * k + 1, 2 * k + 2) for k in range(pairs - 1)]
    swaps += [(b, a) for a, b in swaps]
    mine = lax.dynamic_index_in_dim(x, lax.axis_index("near"), 1, keepdims=False)
    beyond = lax.ppermute(mine, ("far", "near"), swaps)
    def pool_scratch(tiles):
        return (
            pltpu.VMEM((tiles * 64, 128), BF16),
            pltpu.VMEM((tiles, LEVELS, 8, D), F32),
            pltpu.VMEM((tiles * 64, 256), BF16),
        )

    halo_pooled = pltpu.VMEM((LATENT * HALO_TILES * 8, D), BF16)
    gain = first_gain.reshape(1, D)
    latent, attended, spread_query, context = call(
        own_kernel,
        (shaped(TOKENS, D), shaped(HALF, D), shaped(4, 128, 512), shaped(HALF, 2 * D)),
        (*pool_scratch(TILES + HALO_TILES), pltpu.VMEM((LATENT * TILES * 8, D), BF16), halo_pooled,
         pltpu.VMEM((4, 128, 512), BF16)),
        flops=3 * 10**9,
        moved=10**7,
    )(x, folded, folded_bias, expand, latent_query, cross_output, gain, window_query, window_context)
    return call(
        functools.partial(block_kernel, pairs),
        shaped(LATENT, ROWS, COLS, D),
        (*pool_scratch(HALO_TILES), halo_pooled),
        flops=4 * 10**9,
        moved=10**7,
    )(beyond, folded, folded_bias, expand, latent_query, cross_output, gain, window_context, latent, attended,
      spread_query, context, window_output, second_gain.reshape(1, D), up_weight, down_weight)


def solution(mesh):
    finer = Mesh(
        mesh.devices.reshape(mesh.shape["var"], mesh.shape["lat"] // 2, 2, mesh.shape["dp"]),
        ("var", "far", "near", "dp"),
    )
    return jax.shard_map(
        body,
        mesh=finer,
        in_specs=(P(("dp", "var"), ("far", "near"), None),) + (P(),) * 13,
        out_specs=P("dp", ("far", "near"), "var", None),
        check_vma=False,
    )
```

```python
import functools
import math

import jax
import jax.numpy as jnp
from jax import lax
from jax.experimental import pallas as pl
from jax.experimental.pallas import tpu as pltpu
from jax.sharding import Mesh
from jax.sharding import PartitionSpec as P

HEADS = 16
HEAD = 32
D = 512
LATENT = 3
LEVELS = 8
ROWS = 6
COLS = 12
PIXELS = 80
PART = 12
PLACES = 40
HALF = 112
FILLED = 108
TOKENS = 2 * HALF
FOLDED = 608
SCORES = 48
EPSILON = 1e-05
MASKED = -1e30
RATE = HEAD**-0.5 * math.log2(math.e)
F32 = jnp.float32
BF16 = jnp.bfloat16


def dot(a, b):
    return jnp.dot(a, b, preferred_element_type=F32)


def dot_nt(a, b):
    return lax.dot_general(a, b, (((1,), (1,)), ((), ())), preferred_element_type=F32)


def split(a):
    high = a.astype(BF16)
    return high, (a - high.astype(F32)).astype(BF16)


def iota(shape, dim):
    return lax.broadcasted_iota(jnp.int32, shape, dim)


def layer_norm(tensor, scales):
    center = jnp.mean(tensor, axis=-1, keepdims=True)
    offset = tensor - center
    spread = jnp.mean(offset * offset, axis=-1, keepdims=True)
    return offset * lax.rsqrt(spread + EPSILON) * scales


def blocks_kernel(pixels, out, held, wide, rows, staged, arrived, left):
    copy = pltpu.make_async_copy(pixels.at[0], held, arrived)
    copy.start()
    length = held.shape[1]
    wide[:, length:] = jnp.zeros((ROWS, 128), F32)
    copy.wait()
    wide[:, :length] = held[...].astype(F32)
    copies = []
    for v in range(LEVELS):
        for group in range(COLS // 3):
            start = (v * COLS + 3 * group) * PIXELS
            patches = wide[:, start : start + 256]
            rows[v, 3 * group : 3 * group + 3] = patches[:3]
            rows[v, PART + 3 * group : PART + 3 * group + 3] = patches[3:]
        staged[v] = rows[v].astype(BF16)
        for k in range(2):
            copies.append(pltpu.make_async_copy(staged.at[v], out.at[2 * v + k], left.at[2 * v + k]))
            copies[-1].start()
    for copy in copies:
        copy.wait()


def fold_kernel(bias_hbm, embed_hbm, query_hbm, key_hbm, value_hbm, folded, bias, embed, query, key, value, arrived):
    pairs = ((query_hbm, query), (key_hbm, key), (embed_hbm, embed), (value_hbm, value), (bias_hbm, bias))
    copies = [pltpu.make_async_copy(*pair, arrived.at[k]) for k, pair in enumerate(pairs)]
    for copy in copies:
        copy.start()
    for copy in copies:
        copy.wait()
    own = iota((HEADS, D), 1) // HEAD == iota((HEADS, D), 0)
    spread = [jnp.where(own, query[q : q + 1].astype(F32), 0.0) for q in range(LATENT)]
    spread = jnp.concatenate(spread * 2 + [jnp.zeros((128 - 2 * SCORES, D), F32)], axis=0).astype(BF16)
    high, low = split(dot_nt(key[...], spread))
    scores = dot(embed[...], high) + dot(embed[...], low)
    bias_scores = dot(bias[...], high) + dot(bias[...], low)
    high_score, low_score = split(scores)
    lane = iota((1, 128), 1)
    first = jnp.where(lane < SCORES, high_score.astype(F32), low_score.astype(F32))
    bias_high, bias_low = (jnp.where(lane < SCORES, part.astype(F32), 0.0) for part in split(bias_scores))
    value_high, value_low = (part.astype(F32) for part in split(dot(bias[...], value[...])))
    rest = jnp.zeros((128 - PIXELS - 2 * LEVELS, D + 128), F32)
    whole = jnp.concatenate(
        [
            jnp.concatenate([dot(embed[...], value[...]), first], axis=1),
            jnp.concatenate([value_high, bias_high], axis=1),
            jnp.concatenate([value_low, bias_low], axis=1),
            rest,
        ],
        axis=0,
    )
    folded[...] = whole.T[:FOLDED].astype(BF16)


def thirds(lane):
    part = (lane >= PLACES).astype(jnp.int32) + (lane >= 2 * PLACES).astype(jnp.int32)
    return part, lane - PLACES * part


def token_of(place, column):
    group = (place * 171) >> 9
    return (place - 3 * group) * COLS + 3 * group + column


def pick_first(near):
    source = iota((1, LATENT * 128), 1)
    q = source >> 7
    column, place = thirds(source & 127)
    part = (place >= PART).astype(jnp.int32) + (place >= 2 * PART).astype(jnp.int32)
    half = jnp.where(part == 2, 2, jnp.where(part == near, 1, 0))
    token = half * HALF + q * 36 + token_of(place - PART * part, column)
    source = jnp.where((place < 3 * PART) & (column < 3), token, -1)
    source = jnp.where((iota((1, LATENT * 128), 1) & 127) < 3 * PLACES, source, -1)
    target = iota((3 * HALF, 1), 0)
    within = target - HALF * ((target >= HALF).astype(jnp.int32) + (target >= 2 * HALF).astype(jnp.int32))
    target = jnp.where(within >= FILLED, target - (HALF - FILLED), target)
    return jnp.where(source == target, 1.0, 0.0).astype(BF16)


def pick_halo():
    source = iota((1, LATENT * 128), 1)
    q = source >> 7
    _, place = thirds(source & 127)
    column = (place >= PART).astype(jnp.int32) + (place >= 2 * PART).astype(jnp.int32)
    token = q * 36 + token_of(place - PART * column, column)
    source = jnp.where(place < 3 * PART, token, -1)
    source = jnp.where((iota((1, LATENT * 128), 1) & 127) < 3 * PLACES, source, -1)
    target = iota((HALF, 1), 0)
    target = jnp.where(target >= FILLED, target - (HALF - FILLED), target)
    return jnp.where(source == target, 1.0, 0.0).astype(BF16)


def single_patches(x, level):
    lane = iota((1, 128), 1)
    marks = jnp.where((lane == PIXELS + level) | (lane == PIXELS + LEVELS + level), 1.0, 0.0)
    patches = (x[:, :128], x[:, PIXELS : PIXELS + 128], pltpu.roll(x[:, 128:], 256 - 2 * PIXELS, 1))
    return [jnp.where(lane < PIXELS, patch, marks) for patch in patches]


def level_scores(values, step):
    lanes = slice(step * 128, (step + 1) * 128)
    return values[D : D + SCORES, lanes] + values[D + SCORES :, lanes]


def weigh(values, weights, pooled):
    for head in range(HEADS):
        rows = slice(head * HEAD, (head + 1) * HEAD)
        totals = [None] * LATENT
        for step in range(weights.shape[0]):
            value = values[rows, step * 128 : (step + 1) * 128]
            for q in range(LATENT):
                place = q * HEADS + head
                term = value * weights[step, place : place + 1]
                totals[q] = term if step == 0 else totals[q] + term
        for q in range(LATENT):
            pooled[rows, q * 128 : (q + 1) * 128] = totals[q].astype(BF16)


def pool_levels(x, folded, values, weights, pooled):
    values[...] = dot_nt(folded[...], x)
    scores = [level_scores(values, step) for step in range(LEVELS)]
    highest = functools.reduce(jnp.maximum, scores)
    shares = [jnp.exp2((score - highest) * RATE) for score in scores]
    inverse = 1.0 / sum(shares)
    for step in range(LEVELS):
        weights[step] = shares[step] * inverse
    weigh(values, weights, pooled)


def over_parts(a, function):
    lane = iota(a.shape, 1)
    after = jnp.where(lane < 2 * PLACES, pltpu.roll(a, 128 - PLACES, 1), pltpu.roll(a, 2 * PLACES, 1))
    before = jnp.where(lane < PLACES, pltpu.roll(a, 128 - 2 * PLACES, 1), pltpu.roll(a, PLACES, 1))
    return function(function(a, after), before)


def pool_parts(x, folded, values, weights, pooled):
    values[...] = dot_nt(folded[...], x)
    scores = [level_scores(values, step) for step in range(3)]
    scores[2] = jnp.where(iota(scores[2].shape, 1) < 2 * PLACES, scores[2], MASKED)
    highest = over_parts(functools.reduce(jnp.maximum, scores), jnp.maximum)
    shares = [jnp.exp2((score - highest) * RATE) for score in scores]
    inverse = 1.0 / over_parts(sum(shares), jnp.add)
    for step in range(3):
        weights[step] = shares[step] * inverse
    weigh(values, weights, pooled)


def latent_rows(picked, query, output):
    place = iota((HALF, 1), 0)
    first, second, third = (query[q : q + 1].astype(F32) for q in range(LATENT))
    added = jnp.where(place < 36, first, jnp.where(place < 72, second, third))
    added = jnp.concatenate([added] * (picked.shape[0] // HALF), axis=0)
    return (dot(picked.astype(BF16), output[...]) + added).astype(BF16)


def spread_heads(queries, spread):
    part = jnp.concatenate([queries, jnp.zeros((128 - HALF, D), F32)], axis=0).T.astype(BF16)
    spread[...] = jnp.zeros_like(spread)
    for head in range(HEADS):
        group, spot = divmod(head, 4)
        spread[group, spot * HEAD : (spot + 1) * HEAD, spot * 128 : (spot + 1) * 128] = (
            part[head * HEAD : (head + 1) * HEAD]
        )


def attend(spread, own, beside, there):
    lane = iota((1, TOKENS), 1)
    filled = jnp.where(lane >= HALF, lane - HALF, lane) < FILLED
    usable = jnp.where(filled & ((lane < HALF) | there), 1.0, 0.0)
    keys = jnp.concatenate([own[:, :D], jnp.where(there, beside[:, :D], own[:, :D])], axis=0)
    turned = jnp.concatenate([own[:, D:], beside[:, D:]], axis=0).astype(F32).T
    turned = jnp.where(usable > 0.0, turned, 0.0).astype(BF16)
    count = jnp.broadcast_to(usable, (16, TOKENS)).astype(BF16)
    scores = [dot(keys[:, group * 128 : (group + 1) * 128], spread[group]) for group in range(4)]
    shares = [jnp.exp2((score - jnp.max(score, axis=0, keepdims=True)) * RATE).astype(BF16) for score in scores]
    parts = []
    for pair in range(HEADS // 2):
        weighed = jnp.concatenate([turned[pair * 2 * HEAD : (pair + 1) * 2 * HEAD], count], axis=0)
        got = dot(weighed, shares[pair // 2][:, pair % 2 * 256 : (pair % 2 + 1) * 256])
        inverse = 1.0 / got[2 * HEAD : 2 * HEAD + 1]
        parts.append(got[:HEAD, :128] * inverse[:, :128])
        parts.append(got[HEAD : 2 * HEAD, 128:] * inverse[:, 128:])
    return jnp.concatenate(parts, axis=0).T[:HALF].astype(BF16)


def own_kernel(x, folded, query, output, gain, to_query, to_context, latent, attended, spread_query, context,
               rows, values, weights, pooled, spread_here):
    near = lax.axis_index("near")
    for level in range(LEVELS):
        own = x[level, pl.ds(near, 1)].reshape(2 * PART, 256).astype(F32)
        other = x[level, pl.ds(1 - near, 1)].reshape(2 * PART, 256).astype(F32)
        halo = jnp.where(near == 1, other[PART:], other[:PART])
        patches = single_patches(jnp.concatenate([own, halo, jnp.zeros((4, 256), F32)], axis=0), level)
        rows[level] = jnp.concatenate([*patches, jnp.zeros((8, 128), F32)], axis=0).astype(BF16)
    pool_levels(rows[...].reshape(LEVELS * 128, 128), folded, values, weights, pooled)
    picked = dot_nt(pick_first(near), pooled[...])
    tokens = latent_rows(picked, query, output)
    latent[...] = tokens[:TOKENS]
    normed = layer_norm(tokens.astype(F32), gain[...]).astype(BF16)
    queries = dot(normed[:TOKENS], to_query[...]).astype(BF16).astype(F32)
    seen = dot(normed, to_context[...]).astype(BF16)
    context[...] = seen[HALF:TOKENS]
    spread_heads(queries[HALF:], spread_query)
    spread_heads(queries[:HALF], spread_here)
    attended[...] = attend(spread_here, seen[:HALF], seen[TOKENS:], True)


def block_kernel(pairs, beyond, folded, query, output, gain, to_context, latent, attended,
                 spread_query, context, mix, second_gain, up, down, out, rows, values, weights, pooled):
    near = lax.axis_index("near")
    band = lax.axis_index("far") * 2 + near
    for step in range(3):
        parts = []
        for level in range(3 * step, min(3 * step + 3, LEVELS)):
            parts += [*single_patches(beyond[level].astype(F32), level), jnp.zeros((PLACES - 3 * PART, 128), F32)]
        parts.append(jnp.zeros((128 - PLACES * (len(parts) // 4), 128), F32))
        rows[step] = jnp.concatenate(parts, axis=0).astype(BF16)
    pool_parts(rows[...].reshape(3 * 128, 128), folded, values, weights, pooled)
    tokens = latent_rows(dot_nt(pick_halo(), pooled[...]), query, output)
    normed = layer_norm(tokens.astype(F32), gain[...]).astype(BF16)
    beside = dot(normed, to_context[...]).astype(BF16)
    there = (band > 0) & (band < 2 * pairs - 1)
    second_half = attend(spread_query, context[...], beside, there)
    both = jnp.concatenate([attended[...], second_half], axis=0)
    mixed = dot(both, mix[...]) + latent[...].astype(F32)
    second = layer_norm(mixed, second_gain[...]).astype(BF16)
    hidden = jax.nn.gelu(dot(second, up[...])).astype(BF16)
    result = mixed + dot(hidden, down[...])
    for half in range(2):
        first_row = (1 - near if half == 0 else near) * 3
        for q in range(LATENT):
            for i in range(3):
                start = half * HALF + (q * 3 + i) * COLS
                out[q, pl.ds(first_row + i, 1)] = result[start : start + COLS].astype(BF16)[None]


def call(kernel, outs, scratch=(), flops=0, moved=0, limit=24, hbm=0, **specs):
    if hbm:
        specs["in_specs"] = [pl.BlockSpec(memory_space=pltpu.HBM)] * hbm
    return pl.pallas_call(
        kernel,
        out_shape=outs,
        scratch_shapes=list(scratch),
        compiler_params=pltpu.CompilerParams(vmem_limit_bytes=limit * 2**20),
        cost_estimate=pl.CostEstimate(flops=flops, bytes_accessed=moved, transcendentals=0),
        **specs,
    )


def shaped(*shape, dtype=BF16):
    return jax.ShapeDtypeStruct(shape, dtype)


def body(
    patches,
    level_bias,
    embed_weight,
    latent_query,
    cross_key,
    cross_value,
    cross_output,
    first_gain,
    window_query,
    window_context,
    window_output,
    second_gain,
    up_weight,
    down_weight,
):
    pairs = lax.axis_size("far")
    blocks = call(
        blocks_kernel,
        shaped(2 * LEVELS, 2 * PART, 256),
        (
            pltpu.VMEM(patches.shape[1:], BF16),
            pltpu.VMEM((ROWS, patches.shape[2] + 128), F32),
            pltpu.VMEM((LEVELS, 2 * PART, 256), F32),
            pltpu.VMEM((LEVELS, 2 * PART, 256), BF16),
            pltpu.SemaphoreType.DMA,
            pltpu.SemaphoreType.DMA((2 * LEVELS,)),
        ),
        flops=10**6,
        moved=10**6,
        hbm=1,
        out_specs=pl.BlockSpec(memory_space=pl.ANY),
    )(pltpu.with_memory_space_constraint(patches, pltpu.HBM))
    x = lax.all_to_all(blocks, ("var", "near"), 0, 0, tiled=True).reshape(LEVELS, 2, 2 * PART, 256)
    folded = call(
        fold_kernel,
        shaped(FOLDED, 128),
        tuple(pltpu.VMEM(a.shape, BF16) for a in (level_bias, embed_weight, latent_query, cross_key, cross_value))
        + (pltpu.SemaphoreType.DMA((5,)),),
        flops=10**9,
        moved=6 * 10**6,
        hbm=5,
    )(
        *(
            pltpu.with_memory_space_constraint(a, pltpu.HBM)
            for a in (level_bias, embed_weight, latent_query, cross_key, cross_value)
        )
    )
    swaps = [(2 * k + 1, 2 * k + 2) for k in range(pairs - 1)]
    swaps += [(b, a) for a, b in swaps]
    near = lax.axis_index("near")
    mine = lax.dynamic_index_in_dim(x, near, 1, keepdims=False)
    mine = jnp.where(near == 1, mine[:, PART:], mine[:, :PART])
    beyond = lax.ppermute(mine, ("far", "near"), swaps)

    def pool_scratch(steps):
        return (
            pltpu.VMEM((steps, 128, 128), BF16),
            pltpu.VMEM((FOLDED, steps * 128), F32),
            pltpu.VMEM((steps, SCORES, 128), F32),
            pltpu.VMEM((D, LATENT * 128), BF16),
        )

    gain = first_gain.reshape(1, D)
    latent, attended, spread_query, context = call(
        own_kernel,
        (shaped(TOKENS, D), shaped(HALF, D), shaped(4, 128, 512), shaped(HALF, 2 * D)),
        (*pool_scratch(LEVELS), pltpu.VMEM((4, 128, 512), BF16)),
        flops=3 * 10**9,
        moved=10**7,
    )(x, folded, latent_query, cross_output, gain, window_query, window_context)
    return call(
        functools.partial(block_kernel, pairs),
        shaped(LATENT, ROWS, COLS, D),
        pool_scratch(3),
        flops=4 * 10**9,
        moved=10**7,
    )(beyond, folded, latent_query, cross_output, gain, window_context, latent, attended, spread_query, context,
      window_output, second_gain.reshape(1, D), up_weight, down_weight)


def solution(mesh):
    finer = Mesh(
        mesh.devices.reshape(mesh.shape["var"], mesh.shape["lat"] // 2, 2, mesh.shape["dp"]),
        ("var", "far", "near", "dp"),
    )
    return jax.shard_map(
        body,
        mesh=finer,
        in_specs=(P(("dp", "var"), ("far", "near"), None),) + (P(),) * 13,
        out_specs=P("dp", ("far", "near"), "var", None),
        check_vma=False,
    )
```

```python
import functools
import math

import jax
import jax.numpy as jnp
from jax import lax
from jax.experimental import pallas as pl
from jax.experimental.pallas import tpu as pltpu
from jax.sharding import Mesh
from jax.sharding import PartitionSpec as P

HEADS = 16
HEAD = 32
D = 512
LATENT = 3
LEVELS = 8
ROWS = 6
COLS = 12
PIXELS = 80
PART = 12
PLACES = 40
HALF = 112
FILLED = 108
TOKENS = 2 * HALF
FOLDED = 608
SCORES = 48
EPSILON = 1e-05
MASKED = -1e30
RATE = HEAD**-0.5 * math.log2(math.e)
F32 = jnp.float32
BF16 = jnp.bfloat16


def dot(a, b):
    return jnp.dot(a, b, preferred_element_type=F32)


def dot_nt(a, b):
    return lax.dot_general(a, b, (((1,), (1,)), ((), ())), preferred_element_type=F32)


def split(a):
    high = a.astype(BF16)
    return high, (a - high.astype(F32)).astype(BF16)


def iota(shape, dim):
    return lax.broadcasted_iota(jnp.int32, shape, dim)


def layer_norm(tensor, scales):
    center = jnp.mean(tensor, axis=-1, keepdims=True)
    offset = tensor - center
    spread = jnp.mean(offset * offset, axis=-1, keepdims=True)
    return offset * lax.rsqrt(spread + EPSILON) * scales


def blocks_kernel(pixels, out, wide, rows):
    length = pixels.shape[2]
    wide[:, length:] = jnp.zeros((ROWS, 128), F32)
    wide[:, :length] = pixels[0].astype(F32)
    for v in range(LEVELS):
        for group in range(COLS // 3):
            start = (v * COLS + 3 * group) * PIXELS
            patches = wide[:, start : start + 256]
            rows[v, 3 * group : 3 * group + 3] = patches[:3]
            rows[v, PART + 3 * group : PART + 3 * group + 3] = patches[3:]
        block = rows[v].astype(BF16)
        out[2 * v] = block
        out[2 * v + 1] = block


def fold_kernel(bias_hbm, embed_hbm, query_hbm, key_hbm, value_hbm, folded, bias, embed, query, key, value, arrived):
    pairs = ((query_hbm, query), (key_hbm, key), (embed_hbm, embed), (value_hbm, value), (bias_hbm, bias))
    copies = [pltpu.make_async_copy(*pair, arrived.at[k]) for k, pair in enumerate(pairs)]
    for copy in copies:
        copy.start()
    for copy in copies:
        copy.wait()
    own = iota((HEADS, D), 1) // HEAD == iota((HEADS, D), 0)
    spread = [jnp.where(own, query[q : q + 1].astype(F32), 0.0) for q in range(LATENT)]
    spread = jnp.concatenate(spread * 2 + [jnp.zeros((128 - 2 * SCORES, D), F32)], axis=0).astype(BF16)
    high, low = split(dot_nt(key[...], spread))
    scores = dot(embed[...], high) + dot(embed[...], low)
    bias_scores = dot(bias[...], high) + dot(bias[...], low)
    high_score, low_score = split(scores)
    lane = iota((1, 128), 1)
    first = jnp.where(lane < SCORES, high_score.astype(F32), low_score.astype(F32))
    bias_high, bias_low = (jnp.where(lane < SCORES, part.astype(F32), 0.0) for part in split(bias_scores))
    value_high, value_low = (part.astype(F32) for part in split(dot(bias[...], value[...])))
    rest = jnp.zeros((128 - PIXELS - 2 * LEVELS, D + 128), F32)
    whole = jnp.concatenate(
        [
            jnp.concatenate([dot(embed[...], value[...]), first], axis=1),
            jnp.concatenate([value_high, bias_high], axis=1),
            jnp.concatenate([value_low, bias_low], axis=1),
            rest,
        ],
        axis=0,
    )
    folded[...] = whole.T[:FOLDED].astype(BF16)


def thirds(lane):
    part = (lane >= PLACES).astype(jnp.int32) + (lane >= 2 * PLACES).astype(jnp.int32)
    return part, lane - PLACES * part


def token_of(place, column):
    group = (place * 171) >> 9
    return (place - 3 * group) * COLS + 3 * group + column


def pick_first(near):
    source = iota((1, LATENT * 128), 1)
    q = source >> 7
    column, place = thirds(source & 127)
    part = (place >= PART).astype(jnp.int32) + (place >= 2 * PART).astype(jnp.int32)
    half = jnp.where(part == 2, 2, jnp.where(part == near, 1, 0))
    token = half * HALF + q * 36 + token_of(place - PART * part, column)
    source = jnp.where((place < 3 * PART) & (column < 3), token, -1)
    source = jnp.where((iota((1, LATENT * 128), 1) & 127) < 3 * PLACES, source, -1)
    target = iota((3 * HALF, 1), 0)
    within = target - HALF * ((target >= HALF).astype(jnp.int32) + (target >= 2 * HALF).astype(jnp.int32))
    target = jnp.where(within >= FILLED, target - (HALF - FILLED), target)
    return jnp.where(source == target, 1.0, 0.0).astype(BF16)


def pick_halo():
    source = iota((1, LATENT * 128), 1)
    q = source >> 7
    _, place = thirds(source & 127)
    column = (place >= PART).astype(jnp.int32) + (place >= 2 * PART).astype(jnp.int32)
    token = q * 36 + token_of(place - PART * column, column)
    source = jnp.where(place < 3 * PART, token, -1)
    source = jnp.where((iota((1, LATENT * 128), 1) & 127) < 3 * PLACES, source, -1)
    target = iota((HALF, 1), 0)
    target = jnp.where(target >= FILLED, target - (HALF - FILLED), target)
    return jnp.where(source == target, 1.0, 0.0).astype(BF16)


def single_patches(x, level):
    lane = iota((1, 128), 1)
    marks = jnp.where((lane == PIXELS + level) | (lane == PIXELS + LEVELS + level), 1.0, 0.0)
    patches = (x[:, :128], x[:, PIXELS : PIXELS + 128], pltpu.roll(x[:, 128:], 256 - 2 * PIXELS, 1))
    return [jnp.where(lane < PIXELS, patch, marks) for patch in patches]


def level_scores(values, step):
    lanes = slice(step * 128, (step + 1) * 128)
    return values[D : D + SCORES, lanes] + values[D + SCORES :, lanes]


def weigh(values, weights, pooled):
    for head in range(HEADS):
        rows = slice(head * HEAD, (head + 1) * HEAD)
        totals = [None] * LATENT
        for step in range(weights.shape[0]):
            value = values[rows, step * 128 : (step + 1) * 128]
            for q in range(LATENT):
                place = q * HEADS + head
                term = value * weights[step, place : place + 1]
                totals[q] = term if step == 0 else totals[q] + term
        for q in range(LATENT):
            pooled[rows, q * 128 : (q + 1) * 128] = totals[q].astype(BF16)


def pool_levels(x, folded, values, weights, pooled):
    for step in range(LEVELS):
        values[:, step * 128 : (step + 1) * 128] = dot_nt(folded[...], x[step])
    scores = [level_scores(values, step) for step in range(LEVELS)]
    highest = functools.reduce(jnp.maximum, scores)
    shares = [jnp.exp2((score - highest) * RATE) for score in scores]
    inverse = 1.0 / sum(shares)
    for step in range(LEVELS):
        weights[step] = shares[step] * inverse
    weigh(values, weights, pooled)


def over_parts(a, function):
    lane = iota(a.shape, 1)
    after = jnp.where(lane < 2 * PLACES, pltpu.roll(a, 128 - PLACES, 1), pltpu.roll(a, 2 * PLACES, 1))
    before = jnp.where(lane < PLACES, pltpu.roll(a, 128 - 2 * PLACES, 1), pltpu.roll(a, PLACES, 1))
    return function(function(a, after), before)


def pool_parts(x, folded, values, weights, pooled):
    values[...] = dot_nt(folded[...], x)
    scores = [level_scores(values, step) for step in range(3)]
    scores[2] = jnp.where(iota(scores[2].shape, 1) < 2 * PLACES, scores[2], MASKED)
    highest = over_parts(functools.reduce(jnp.maximum, scores), jnp.maximum)
    shares = [jnp.exp2((score - highest) * RATE) for score in scores]
    inverse = 1.0 / over_parts(sum(shares), jnp.add)
    for step in range(3):
        weights[step] = shares[step] * inverse
    weigh(values, weights, pooled)


def latent_rows(picked, query, output):
    place = iota((HALF, 1), 0)
    first, second, third = (query[q : q + 1].astype(F32) for q in range(LATENT))
    added = jnp.where(place < 36, first, jnp.where(place < 72, second, third))
    added = jnp.concatenate([added] * (picked.shape[0] // HALF), axis=0)
    return (dot(picked.astype(BF16), output[...]) + added).astype(BF16)


def spread_heads(queries, spread):
    part = jnp.concatenate([queries, jnp.zeros((128 - HALF, D), F32)], axis=0).T.astype(BF16)
    spread[...] = jnp.zeros_like(spread)
    for head in range(HEADS):
        group, spot = divmod(head, 4)
        spread[group, spot * HEAD : (spot + 1) * HEAD, spot * 128 : (spot + 1) * 128] = (
            part[head * HEAD : (head + 1) * HEAD]
        )


def attend(spread, own, beside, there):
    lane = iota((1, TOKENS), 1)
    filled = jnp.where(lane >= HALF, lane - HALF, lane) < FILLED
    usable = jnp.where(filled & ((lane < HALF) | there), 1.0, 0.0)
    keys = jnp.concatenate([own[:, :D], jnp.where(there, beside[:, :D], own[:, :D])], axis=0)
    turned = jnp.concatenate([own[:, D:], beside[:, D:]], axis=0).astype(F32).T
    turned = jnp.where(usable > 0.0, turned, 0.0).astype(BF16)
    count = jnp.broadcast_to(usable, (16, TOKENS)).astype(BF16)
    scores = [dot(keys[:, group * 128 : (group + 1) * 128], spread[group]) for group in range(4)]
    shares = [jnp.exp2((score - jnp.max(score, axis=0, keepdims=True)) * RATE).astype(BF16) for score in scores]
    parts = []
    for pair in range(HEADS // 2):
        weighed = jnp.concatenate([turned[pair * 2 * HEAD : (pair + 1) * 2 * HEAD], count], axis=0)
        got = dot(weighed, shares[pair // 2][:, pair % 2 * 256 : (pair % 2 + 1) * 256])
        inverse = 1.0 / got[2 * HEAD : 2 * HEAD + 1]
        parts.append(got[:HEAD, :128] * inverse[:, :128])
        parts.append(got[HEAD : 2 * HEAD, 128:] * inverse[:, 128:])
    return jnp.concatenate(parts, axis=0).T[:HALF].astype(BF16)


def own_kernel(x, folded, query, output, gain, to_query, to_context, latent, attended, spread_query, context,
               rows, values, weights, pooled, spread_here):
    near = lax.axis_index("near")
    for level in range(LEVELS):
        own = x[level, pl.ds(near, 1)].reshape(2 * PART, 256).astype(F32)
        other = x[level, pl.ds(1 - near, 1)].reshape(2 * PART, 256).astype(F32)
        halo = jnp.where(near == 1, other[PART:], other[:PART])
        patches = single_patches(jnp.concatenate([own, halo, jnp.zeros((4, 256), F32)], axis=0), level)
        rows[level] = jnp.concatenate([*patches, jnp.zeros((8, 128), F32)], axis=0).astype(BF16)
    pool_levels(rows, folded, values, weights, pooled)
    picked = dot_nt(pick_first(near), pooled[...])
    tokens = latent_rows(picked, query, output)
    latent[...] = tokens[:TOKENS]
    normed = layer_norm(tokens.astype(F32), gain[...]).astype(BF16)
    queries = dot(normed[:TOKENS], to_query[...]).astype(BF16).astype(F32)
    seen = dot(normed, to_context[...]).astype(BF16)
    context[...] = seen[HALF:TOKENS]
    spread_heads(queries[HALF:], spread_query)
    spread_heads(queries[:HALF], spread_here)
    attended[...] = attend(spread_here, seen[:HALF], seen[TOKENS:], True)


def block_kernel(pairs, beyond, folded, query, output, gain, to_context, latent, attended,
                 spread_query, context, mix, second_gain, up, down, out, rows, values, weights, pooled, staged, left):
    near = lax.axis_index("near")
    band = lax.axis_index("far") * 2 + near
    wide = beyond[...].astype(F32)
    for step in range(3):
        parts = []
        for level in range(3 * step, min(3 * step + 3, LEVELS)):
            parts += [*single_patches(wide[level * PART : (level + 1) * PART], level), jnp.zeros((PLACES - 3 * PART, 128), F32)]
        parts.append(jnp.zeros((128 - PLACES * (len(parts) // 4), 128), F32))
        rows[step] = jnp.concatenate(parts, axis=0).astype(BF16)
    pool_parts(rows[...].reshape(3 * 128, 128), folded, values, weights, pooled)
    tokens = latent_rows(dot_nt(pick_halo(), pooled[...]), query, output)
    normed = layer_norm(tokens.astype(F32), gain[...]).astype(BF16)
    beside = dot(normed, to_context[...]).astype(BF16)
    there = (band > 0) & (band < 2 * pairs - 1)
    second_half = attend(spread_query, context[...], beside, there)
    both = jnp.concatenate([attended[...], second_half], axis=0)
    mixed = dot(both, mix[...]) + latent[...].astype(F32)
    second = layer_norm(mixed, second_gain[...]).astype(BF16)
    copies = []
    for half in range(2):
        own = slice(half * HALF, (half + 1) * HALF)
        hidden = jax.nn.gelu(dot(second[own], up[...])).astype(BF16)
        result = mixed[own] + dot(hidden, down[...])
        for q in range(LATENT):
            for i in range(3):
                start = (q * 3 + i) * COLS
                staged[half, q, i] = result[start : start + COLS].astype(BF16)
        first_row = 3 - 3 * near if half == 0 else 3 * near
        copies.append(pltpu.make_async_copy(staged.at[half], out.at[:, pl.ds(first_row, 3)], left.at[half]))
        copies[-1].start()
    for copy in copies:
        copy.wait()


def call(kernel, outs, scratch=(), flops=0, moved=0, limit=24, hbm=0, **specs):
    if hbm:
        specs["in_specs"] = [pl.BlockSpec(memory_space=pltpu.HBM)] * hbm
    return pl.pallas_call(
        kernel,
        out_shape=outs,
        scratch_shapes=list(scratch),
        compiler_params=pltpu.CompilerParams(vmem_limit_bytes=limit * 2**20),
        cost_estimate=pl.CostEstimate(flops=flops, bytes_accessed=moved, transcendentals=0),
        **specs,
    )


def shaped(*shape, dtype=BF16):
    return jax.ShapeDtypeStruct(shape, dtype)


def body(
    patches,
    level_bias,
    embed_weight,
    latent_query,
    cross_key,
    cross_value,
    cross_output,
    first_gain,
    window_query,
    window_context,
    window_output,
    second_gain,
    up_weight,
    down_weight,
):
    pairs = lax.axis_size("far")
    blocks = call(
        blocks_kernel,
        shaped(2 * LEVELS, 2 * PART, 256),
        (pltpu.VMEM((ROWS, patches.shape[2] + 128), F32), pltpu.VMEM((LEVELS, 2 * PART, 256), F32)),
        flops=10**6,
        moved=10**6,
    )(patches)
    x = lax.all_to_all(blocks, ("var", "near"), 0, 0, tiled=True).reshape(LEVELS, 2, 2 * PART, 256)
    folded = call(
        fold_kernel,
        shaped(FOLDED, 128),
        tuple(pltpu.VMEM(a.shape, BF16) for a in (level_bias, embed_weight, latent_query, cross_key, cross_value))
        + (pltpu.SemaphoreType.DMA((5,)),),
        flops=10**9,
        moved=6 * 10**6,
        hbm=5,
    )(
        *(
            pltpu.with_memory_space_constraint(a, pltpu.HBM)
            for a in (level_bias, embed_weight, latent_query, cross_key, cross_value)
        )
    )
    swaps = [(2 * k + 1, 2 * k + 2) for k in range(pairs - 1)]
    swaps += [(b, a) for a, b in swaps]
    near = lax.axis_index("near")
    mine = lax.dynamic_index_in_dim(x, near, 1, keepdims=False)
    mine = jnp.where(near == 1, mine[:, PART:], mine[:, :PART]).reshape(LEVELS * PART, 256)
    beyond = lax.ppermute(mine, ("far", "near"), swaps)

    def pool_scratch(steps):
        return (
            pltpu.VMEM((steps, 128, 128), BF16),
            pltpu.VMEM((FOLDED, steps * 128), F32),
            pltpu.VMEM((steps, SCORES, 128), F32),
            pltpu.VMEM((D, LATENT * 128), BF16),
        )

    gain = first_gain.reshape(1, D)
    latent, attended, spread_query, context = call(
        own_kernel,
        (shaped(TOKENS, D), shaped(HALF, D), shaped(4, 128, 512), shaped(HALF, 2 * D)),
        (*pool_scratch(LEVELS), pltpu.VMEM((4, 128, 512), BF16)),
        flops=3 * 10**9,
        moved=10**7,
    )(x, folded, latent_query, cross_output, gain, window_query, window_context)
    return call(
        functools.partial(block_kernel, pairs),
        shaped(LATENT, ROWS, COLS, D),
        (*pool_scratch(3), pltpu.VMEM((2, LATENT, 3, COLS, D), BF16), pltpu.SemaphoreType.DMA((2,))),
        flops=4 * 10**9,
        moved=10**7,
        out_specs=pl.BlockSpec(memory_space=pl.ANY),
    )(beyond, folded, latent_query, cross_output, gain, window_context, latent, attended, spread_query, context,
      window_output, second_gain.reshape(1, D), up_weight, down_weight)


def solution(mesh):
    finer = Mesh(
        mesh.devices.reshape(mesh.shape["var"], mesh.shape["lat"] // 2, 2, mesh.shape["dp"]),
        ("var", "far", "near", "dp"),
    )
    return jax.shard_map(
        body,
        mesh=finer,
        in_specs=(P(("dp", "var"), ("far", "near"), None),) + (P(),) * 13,
        out_specs=P("dp", ("far", "near"), "var", None),
        check_vma=False,
    )
```
